256 devices in a mesh: struct: 64 (over y, z, core), feat: 4 (over x).
Axes of the slice: x: 4, y: 4, z: 8, core: 2. Of those that a mesh axis runs over, the one named last changes fastest.
Arguments:
- descriptors: bfloat16 [98304, 512], P('struct', 'feat'), may hold values from -1 to 1, as said below
- atom_counts: int32 [64, 32], P('struct'), may hold values from 1 to 128, 1536 in all within a row
- partner_requests: int32 [4096], P('struct'), may hold values from 0 to 31
- pair_local: int32 [98304], P('struct'), may hold values from 0 to 31
- pair_slot: int32 [98304], P('struct'), may hold values from 0 to 63
Outputs:
- weights: float32 [98304], P(('struct', 'feat'))
The draws below stay inside these ranges and needn't reach their ends.
Inputs may be any that keep to these rules, and one draw needn't show every extreme that they name: Each row holds real-valued descriptors. `partner_requests`: entry r of a struct index's 64 requests names a structure held by struct index r. `pair_slot`: indexes the 64 requests of the pair's own struct index.
All inputs are finite; a program needn't handle non-finite values.
Results may differ from the reference program's by a relative error of at most 0.0003.
Values may be sent and summed in bfloat16 or wider, within the bound.
A program may use at most 128 MiB of HBM per device.

```python
import math
import jax
import jax.numpy as jnp
import numpy as np
from jax import lax

D = 512
MAXAT = 128
STRUCT_DEV = 32
R_DEV = 64
PAIR_DEV = 1536
ATOM_DEV = 1536
ATOMS = 98304
SLOT = 1
REQUESTS = 4096
PAIRS = 98304
N_STRUCT = 64
N_FEAT = 4


def draw_descriptors(key, part):
    key = jax.random.fold_in(key, 7)
    key_mean, key_level, key_noise = jax.random.split(key, 3)
    common = jax.random.normal(key_mean, (1, D), jnp.float32) / jnp.sqrt(jnp.float32(D))
    level = jax.random.uniform(key_level, (ATOMS, 1), jnp.float32, 0.2, 1.0)
    noise = jax.random.normal(key_noise, (ATOMS, D), jnp.float32) / jnp.sqrt(jnp.float32(D))
    values = jnp.clip(level * common + noise, -1.0, 1.0)
    return values.astype(jnp.bfloat16)


def set_ends(result, key, least, largest):
    longest = result.shape.index(max(result.shape))
    spots = []
    for shift in (0, 1):
        where = [jax.random.randint(jax.random.fold_in(key, axis), (), 0, length) for axis, length in enumerate(result.shape)]
        where[longest] = (where[longest] + shift) % result.shape[longest]
        spots.append(tuple(where))
    return result.at[spots[0]].set(least).at[spots[1]].set(largest)


def profile(number_of, total, most, lean):
    weights = [(1 << 20) // math.isqrt(rank ** lean) + 1 for rank in range(2, number_of + 1)]
    rest, holding = total - most - (number_of - 1), [1] * (number_of - 1)
    while rest > 0:
        movable = [i for i in range(number_of - 1) if holding[i] < most]
        whole, left = sum([weights[i] for i in movable]), rest
        for i in movable:
            more = min(most - holding[i], max(1, left * weights[i] // whole), rest)
            holding[i] = holding[i] + more
            rest = rest - more
    return np.array([most] + holding)


def ragged_sizes(own_key, number_of, total, most, skew):
    if number_of == 2:
        one = jax.random.randint(own_key, (), max(1, total - most), min(most, total - 1) + 1)
        return jnp.stack([one, total - one])
    lengths = jnp.asarray(profile(number_of, total, most, skew), jnp.int32)
    couples = (number_of - 1) // 2
    giver, taker = lengths[1:1 + 2 * couples:2], lengths[2:2 + 2 * couples:2]
    slack = jnp.minimum(giver - 1, most - taker)
    passed = jax.random.randint(jax.random.fold_in(own_key, 1), (couples,), 0, 1 << 20) % (slack + 1)
    lengths = lengths.at[1:1 + 2 * couples:2].set(giver - passed).at[2:2 + 2 * couples:2].set(taker + passed)
    return lengths[jax.random.permutation(jax.random.fold_in(own_key, 2), number_of)]


def setup_inputs(seed: int = 0) -> dict:
    splits = jax.random.split(jax.random.key(seed), 6)
    return {
        "descriptors": draw_descriptors(jax.random.fold_in(splits[5], 71), 0),
        "atom_counts": jax.vmap(lambda own: ragged_sizes(own, STRUCT_DEV, ATOM_DEV, MAXAT, 2))(jax.random.split(splits[1], N_STRUCT)).reshape((N_STRUCT, STRUCT_DEV)).astype(jnp.int32),
        "partner_requests": set_ends(jax.random.randint(splits[2], (REQUESTS,), 0, STRUCT_DEV), jax.random.fold_in(splits[2], 1), 0, STRUCT_DEV - 1).astype(jnp.int32),
        "pair_local": set_ends(jax.random.randint(splits[3], (PAIRS,), 0, STRUCT_DEV), jax.random.fold_in(splits[3], 1), 0, STRUCT_DEV - 1).astype(jnp.int32),
        "pair_slot": set_ends(jax.random.randint(splits[4], (PAIRS,), 0, R_DEV), jax.random.fold_in(splits[4], 1), 0, R_DEV - 1).astype(jnp.int32),
    }


def pack_rows(flat, starts, counts):
    offsets = jnp.arange(MAXAT, dtype=jnp.int32)
    row_ids = starts[:, None] + offsets[None, :]
    in_range = offsets[None, :] < counts[:, None]
    gathered_rows = jnp.take(flat, jnp.clip(row_ids, 0, flat.shape[0] - 1).astype(jnp.int32), axis=0)
    return jnp.where(in_range[:, :, None], gathered_rows, jnp.zeros_like(gathered_rows))

def square_sums(left_rows, right_rows):
    products = jnp.einsum('amd,and->amn', left_rows.astype(jnp.float32), right_rows.astype(jnp.float32))
    return lax.optimization_barrier(jnp.sum(products * products, axis=(1, 2)))

def reference(descriptors, atom_counts, partner_requests, pair_local, pair_slot):
    counts = atom_counts.astype(jnp.int32)
    base_rows = (jnp.arange(N_STRUCT, dtype=jnp.int32) * ATOM_DEV)[:, None]
    starts = (jnp.cumsum(counts, axis=1) - counts + base_rows).astype(jnp.int32)

    def own_self(device):
        packed = pack_rows(descriptors, starts[device], counts[device])
        return square_sums(packed, packed)
    self_kernel = lax.map(own_self, jnp.arange(N_STRUCT, dtype=jnp.int32))
    self_flat = self_kernel.reshape(-1)
    starts_flat = starts.reshape(-1)
    counts_flat = counts.reshape(-1)

    def device_weights(device):
        local_tiles = pack_rows(descriptors, starts[device], counts[device])
        wanted = lax.dynamic_slice_in_dim(partner_requests, device * R_DEV, R_DEV)
        holder = jnp.arange(R_DEV, dtype=jnp.int32) // SLOT
        partner_ids = (holder * STRUCT_DEV + wanted).astype(jnp.int32)
        partner = pack_rows(descriptors, starts_flat[partner_ids], counts_flat[partner_ids])
        pair_rows = lax.dynamic_slice_in_dim(pair_local, device * PAIR_DEV, PAIR_DEV)
        slot_rows = lax.dynamic_slice_in_dim(pair_slot, device * PAIR_DEV, PAIR_DEV)

        def block_sums(index_pair):
            return square_sums(local_tiles[index_pair[0]], partner[index_pair[1]])
        cross_sums = lax.map(block_sums, (pair_rows.reshape(N_FEAT, -1), slot_rows.reshape(N_FEAT, -1))).reshape(-1)
        left_self = self_kernel[device][pair_rows]
        right_self = self_flat[partner_ids][slot_rows]
        return cross_sums / jnp.sqrt(left_self * right_self)
    weights = lax.map(device_weights, jnp.arange(N_STRUCT, dtype=jnp.int32))
    return weights.reshape(-1)
```

```python
import jax
import jax.numpy as jnp
from jax import lax
from jax.experimental import pallas as pl
from jax.experimental.pallas import tpu as pltpu
from jax.sharding import PartitionSpec as P

MAXAT = 128
ATOMS_DEV = 1536
STRUCTS = 32
F = 4
NY, NZ, NC = 4, 8, 2
FEATS = 128
DEPTH = F * FEATS
ROWS = ATOMS_DEV // F
TILE = MAXAT // F
SPOTS = NY * NC
CHUNKS = 4
CHUNK = ROWS // CHUNKS
PAIRS = 384
MESH = pl.DeviceIdType.MESH
BF16, F32 = jnp.bfloat16, jnp.float32

NEAR = [(dy, dc) for dy in range(NY) for dc in range(NC)]
NT = (((1,), (1,)), ((), ()))


def iota(shape, dim):
    return lax.broadcasted_iota(jnp.int32, shape, dim)


def fiota(shape, dim):
    return iota(shape, dim).astype(F32)


def dot(a, b):
    return jnp.dot(a, b, preferred_element_type=F32)


def split3(x):
    high = x.astype(BF16)
    rest = x - high.astype(F32)
    middle = rest.astype(BF16)
    return high, middle, (rest - middle.astype(F32)).astype(BF16)


def kernel(x_ref, counts_ref, req_ref, local_ref, slot_ref, out_ref,
           rows, ring, stage, recv, info, asked, sizes, sums, own_self, near_self, plane_self,
           far_self, table, tables,
           x_send, x_recv, xr_send, xr_recv, z_send, z_recv, a_send, a_recv, c_send, c_recv,
           y_send, y_recv, s_send, s_recv, p_send, p_recv, t_send, t_recv):
    s = lax.axis_index("struct")
    f = lax.axis_index("feat")
    y, z, c = s // (NZ * NC), lax.rem(s // NC, NZ), lax.rem(s, NC)
    ff = f.astype(F32)

    def struct_at(dz, dy, dc):
        return (lax.rem(y + dy + NY, NY) * NZ + lax.rem(z + dz + NZ, NZ)) * NC + lax.rem(c + dc, NC)

    def at(dz, dy, dc):
        return {"struct": struct_at(dz, dy, dc)}

    def copy(src, dst, send, recv_sem, to):
        made = pltpu.make_async_remote_copy(
            src_ref=src, dst_ref=dst, send_sem=send, recv_sem=recv_sem, device_id=to,
            device_id_type=MESH)
        made.start()
        return made

    sent = []
    peers = [at(0, dy, dc) for dy, dc in NEAR[1:]]
    peers += [at(dz, dy, dc) for dz in (1, -1) for dy, dc in NEAR]
    peers += [at(dz, 0, 0) for dz in (2, 3, 4, -3, -2)]
    peers += [{"feat": lax.rem(f + d, F)} for d in range(1, F)]
    barrier = pltpu.get_barrier_semaphore()
    for peer in peers:
        pl.semaphore_signal(barrier, inc=1, device_id=peer, device_id_type=MESH)

    step = 2 * FEATS
    part = step // F
    r, q = iota((step, step), 0), iota((step, step), 1)
    wanted = F * lax.rem(r, part) + lax.rem(r // part + f, F)
    deal = jnp.where(q == wanted, 1.0, 0.0).astype(BF16)
    for b in range(ATOMS_DEV // step):
        dealt = dot(deal, x_ref[b * step:(b + 1) * step, :]).astype(BF16)
        for e in range(F):
            rows[e, b * part:(b + 1) * part, 0:FEATS] = dealt[e * part:(e + 1) * part, :]

    counts_row = jnp.concatenate(
        [counts_ref[...].astype(F32), jnp.zeros((1, 128 - STRUCTS), F32)], axis=1)
    req_row = jnp.concatenate(
        [req_ref[...].reshape(1, NY * NZ * NC).astype(F32), jnp.zeros((1, 64), F32)], axis=1)
    sub, lane = iota((STRUCTS, 128), 0), iota((STRUCTS, 128), 1)
    counts_col = jnp.sum(jnp.where(sub == lane, counts_row, 0.0), axis=1, keepdims=True)
    starts_row = jnp.sum(jnp.where(sub < lane, counts_col, 0.0), axis=0, keepdims=True)
    starts_col = jnp.sum(jnp.where(lane < sub, counts_row, 0.0), axis=1, keepdims=True)
    info[...] = jnp.concatenate(
        [req_row, counts_row, starts_row, jnp.zeros((5, 128), F32)], axis=0)

    pl.semaphore_wait(barrier, len(peers))

    first = {}
    for ch in range(CHUNKS):
        part_rows = pl.ds(ch * CHUNK, CHUNK)
        for d in range(1, F):
            first[d, ch] = copy(
                rows.at[d, part_rows, pl.ds(0, FEATS)],
                rows.at[0, part_rows, pl.ds((F - d) * FEATS, FEATS)],
                x_send.at[d - 1, ch], x_recv.at[d - 1, ch], {"feat": lax.rem(f + d, F)})
    asks = {}
    for dz, spots in ((0, range(1, SPOTS)), (1, range(0, SPOTS, 2)), (-1, range(1, SPOTS, 2))):
        for t in spots:
            dy, dc = NEAR[t]
            asks[dz, t] = copy(info, asked.at[dz % 3, t], a_send.at[dz % 3, t], a_recv.at[dz % 3, t],
                               at(-dz, -dy, dc))
    size_copies = {}
    for o in (1, 2, 3, 5, 6, 7):
        size_copies[o] = copy(info, sizes.at[o], c_send.at[o], c_recv.at[o], at(o, 0, 0))
    rest = {}
    for e in range(1, F):
        for d in range(1, F):
            rest[d, e] = copy(
                rows.at[(e + d) % F, :, pl.ds(0, FEATS)],
                rows.at[e, :, pl.ds((F - d) * FEATS, FEATS)],
                xr_send.at[d - 1, e - 1], xr_recv.at[d - 1, e - 1], {"feat": lax.rem(f + d, F)})

    hops = {}

    def hop(o, to, ch):
        src = rows.at[0] if o == 0 else ring.at[o]
        dst = (o + to) % NZ
        part_rows = pl.ds(ch * CHUNK, CHUNK)
        hops[dst, ch] = copy(src.at[part_rows], ring.at[dst, part_rows],
                             z_send.at[dst, ch], z_recv.at[dst, ch], at(to, 0, 0))

    for ch in range(CHUNKS):
        for d in range(1, F):
            first[d, ch].wait_recv()
        hop(0, 1, ch)
        hop(0, -1, ch)

    for t in range(1, SPOTS):
        asks[0, t].wait_recv()
    near_asks = jnp.concatenate([info[0:1, :]] + [asked[0, t, 0:1, :] for t in range(1, SPOTS)], axis=0)

    def cut(block, sizes_ref, o, asks_rows):
        n = asks_rows.shape[0]
        lanes = iota((n, 128), 1)
        holder = struct_at(-o, 0, 0)
        asked_for = jnp.sum(jnp.where(lanes == holder, asks_rows, 0.0), axis=1, keepdims=True)
        chosen = lanes.astype(F32) == asked_for
        count = jnp.sum(jnp.where(chosen, sizes_ref[1:2, :], 0.0), axis=1, keepdims=True)
        start = jnp.sum(jnp.where(chosen, sizes_ref[2:3, :], 0.0), axis=1, keepdims=True)
        begin = jnp.floor((start - ff + 3.0) * 0.25)
        end = jnp.floor((start + count - ff + 3.0) * 0.25)
        begin = jnp.broadcast_to(begin, (n, ROWS))
        end = jnp.broadcast_to(end, (n, ROWS))
        i, k = fiota((TILE, ROWS), 0), fiota((TILE, ROWS), 1)
        picks = [jnp.where((begin[t:t + 1] + i == k) & (k < end[t:t + 1]), 1.0, 0.0).astype(BF16)
                 for t in range(n)]
        return dot(jnp.concatenate(picks, axis=0), block).astype(BF16)

    tiles = {}

    def serve(o):
        block = rows[0] if o == 0 else ring[o]
        if o not in (0, 3, 5):
            size_copies[o].wait_recv()
        made = cut(block, info if o == 0 else sizes.at[o], o, near_asks)
        stage[o] = made
        recv[o, 0:TILE, :] = made[0:TILE, :]
        for t in range(1, SPOTS):
            dy, dc = NEAR[t]
            part_rows = pl.ds(t * TILE, TILE)
            tiles[o, t] = copy(stage.at[o, part_rows], recv.at[o, part_rows],
                               y_send.at[o, t], y_recv.at[o, t], at(0, dy, dc))

    def serve_far(o, dz):
        spots = range(0, SPOTS, 2) if dz == 1 else range(1, SPOTS, 2)
        for t in spots:
            asks[dz, t].wait_recv()
        far_asks = jnp.concatenate([asked[dz % 3, t, 0:1, :] for t in spots], axis=0)
        size_copies[o].wait_recv()
        made = cut(ring[o], sizes.at[o], o, far_asks)
        for n, t in enumerate(spots):
            part_rows = pl.ds(t * TILE, TILE)
            dy, dc = NEAR[t]
            stage[4, part_rows, :] = made[n * TILE:(n + 1) * TILE, :]
            tiles[4, t] = copy(stage.at[4, part_rows], recv.at[4, part_rows],
                               y_send.at[4, t], y_recv.at[4, t], at(dz, dy, dc))

    def products(o):
        for t in range(0 if o == 4 else 1, SPOTS):
            tiles[o, t].wait_recv()

        def one(e, carry):
            p = lax.dot_general(recv[o], rows[e], NT, preferred_element_type=F32)
            sums[e, o * SPOTS:(o + 1) * SPOTS, :] = jnp.sum(
                (p * p).reshape(SPOTS, TILE, ROWS), axis=1)
            return carry

        lax.fori_loop(0, F, one, 0)

    serve(0)
    for o in (1, 2):
        for ch in range(CHUNKS):
            hops[o, ch].wait_recv()
            hop(o, 1, ch)
            hops[NZ - o, ch].wait_recv()
            hop(NZ - o, -1, ch)
        serve(o)
        serve(NZ - o)

    for copied in rest.values():
        copied.wait_recv()

    ends_row = starts_row + counts_row
    own_row = F * fiota((ROWS, 128), 0) + ff
    own_seg = jnp.sum(jnp.where((ends_row <= own_row) & (iota((ROWS, 128), 1) < STRUCTS), 1.0, 0.0),
                      axis=1, keepdims=True)

    def members(e):
        index = F * iota((STRUCTS, ROWS), 1) + lax.rem(f + e, F)
        index = index.astype(F32)
        return (starts_col <= index) & (index < starts_col + counts_col)

    def self_part(e, total):
        inside = members(e)
        seg = jnp.sum(jnp.where(inside, fiota((STRUCTS, ROWS), 0), 0.0), axis=0, keepdims=True)
        p = lax.dot_general(rows[0], rows[e], NT, preferred_element_type=F32)
        p = jnp.where(own_seg == seg, p, 0.0)
        by_column = jnp.sum(p * p, axis=0, keepdims=True)
        return total + jnp.sum(jnp.where(inside, by_column, 0.0), axis=1, keepdims=True)

    self_col = lax.fori_loop(0, F, self_part, jnp.zeros((STRUCTS, 1), F32))
    self_row = jnp.sum(jnp.where(sub == lane, self_col, 0.0), axis=0, keepdims=True)
    own_self[...] = jnp.broadcast_to(self_row, (8, 128))
    self_copies = {}
    for t in range(1, SPOTS):
        dy, dc = NEAR[t]
        self_copies[t] = copy(own_self, near_self.at[t], s_send.at[t], s_recv.at[t], at(0, dy, dc))

    products(0)
    for t in range(1, SPOTS):
        self_copies[t].wait_recv()
    plane_self[...] = jnp.concatenate(
        [own_self[0:1, :]] + [near_self[t, 0:1, :] for t in range(1, SPOTS)], axis=0)
    plane_copies = {}
    for o in range(1, NZ):
        plane_copies[o] = copy(plane_self, far_self.at[o], p_send.at[o], p_recv.at[o], at(o, 0, 0))
    products(1)
    products(7)

    for ch in range(CHUNKS):
        hops[3, ch].wait_recv()
    serve_far(3, 1)
    for ch in range(CHUNKS):
        hops[5, ch].wait_recv()
    serve_far(5, -1)
    serve(3)
    serve(5)
    products(2)
    products(6)

    holders = NZ * SPOTS
    spot = iota((holders, 128), 0)
    o_of, t_of = spot // SPOTS, lax.rem(spot, SPOTS)
    holder_col = (lax.rem(y - t_of // NC + NY, NY) * NZ + lax.rem(z - o_of + NZ, NZ)) * NC + lax.rem(
        c + lax.rem(t_of, NC), NC)
    lanes = iota((holders, 128), 1)
    my_request = jnp.sum(jnp.where(lanes == holder_col, info[0:1, :], 0.0), axis=1, keepdims=True)
    for o in range(1, NZ):
        plane_copies[o].wait_recv()
    all_self = jnp.concatenate([plane_self[...]] + [far_self[o] for o in range(1, NZ)], axis=0)
    partner_self = jnp.sum(jnp.where(lanes.astype(F32) == my_request, all_self, 0.0), axis=1, keepdims=True)
    partner_row = jnp.sum(jnp.where(lanes == spot, partner_self, 0.0), axis=0, keepdims=True)

    products(3)
    products(5)
    products(4)

    def by_structure(e, total):
        inside = jnp.where(members(e), 1.0, 0.0).astype(BF16)
        for piece in split3(sums[e]):
            total = total + lax.dot_general(inside, piece, NT, preferred_element_type=F32)
        return total

    cross = lax.fori_loop(0, F, by_structure, jnp.zeros((STRUCTS, holders), F32))
    cross = jnp.concatenate([cross, jnp.broadcast_to(self_col, (STRUCTS, 128 - holders))], axis=1)
    table[...] = jnp.concatenate([cross, jnp.broadcast_to(partner_row, (8, 128))], axis=0)
    table_copies = [
        copy(table, tables.at[d - 1], t_send.at[d - 1], t_recv.at[d - 1], {"feat": lax.rem(f + d, F)})
        for d in range(1, F)]

    slot = slot_ref[pl.ds(pl.multiple_of(f * PAIRS, 128), PAIRS)].reshape(1, PAIRS)
    local = local_ref[pl.ds(pl.multiple_of(f * PAIRS, 128), PAIRS)].reshape(1, PAIRS)
    spot = iota((128, PAIRS), 0)
    o_of, t_of = spot // SPOTS, lax.rem(spot, SPOTS)
    holder_col = (lax.rem(y - t_of // NC + NY, NY) * NZ + lax.rem(z + NZ - lax.rem(o_of, NZ), NZ)) * NC + lax.rem(
        c + lax.rem(t_of, NC), NC)
    slot_pick = jnp.where((holder_col == slot) & (spot < holders), 1.0, 0.0).astype(BF16)
    local_pick = iota((STRUCTS, PAIRS), 0) == local

    for copied in table_copies:
        copied.wait_recv()
    total = (table[...] + tables[0]) + (tables[1] + tables[2])
    picked = sum(dot(piece, slot_pick) for piece in split3(total))
    left_self = jnp.sum(jnp.where(local_pick, total[0:STRUCTS, holders:holders + 1], 0.0), axis=0, keepdims=True)
    value = jnp.sum(jnp.where(local_pick, picked[0:STRUCTS], 0.0), axis=0, keepdims=True)
    right_self = picked[STRUCTS:STRUCTS + 1]
    out_ref[...] = (value / jnp.sqrt(left_self * right_self)).reshape(PAIRS)

    for copied in (*first.values(), *rest.values(), *asks.values(), *size_copies.values(), *hops.values(),
                   *tiles.values(), *self_copies.values(), *plane_copies.values(), *table_copies):
        copied.wait_send()


def per_device(descriptors, atom_counts, partner_requests, pair_local, pair_slot):
    dma = pltpu.SemaphoreType.DMA
    vmem = pltpu.VMEM
    pairs_of = lambda shape: [dma(shape), dma(shape)]
    return pl.pallas_call(
        kernel,
        out_shape=jax.ShapeDtypeStruct((PAIRS,), F32),
        in_specs=[pl.BlockSpec(memory_space=vmem)] * 5,
        out_specs=pl.BlockSpec(memory_space=vmem),
        scratch_shapes=[
            vmem((F, ROWS, DEPTH), BF16),
            vmem((NZ, ROWS, DEPTH), BF16),
            vmem((NZ, SPOTS * TILE, DEPTH), BF16),
            vmem((NZ, SPOTS * TILE, DEPTH), BF16),
            vmem((8, 128), F32),
            vmem((3, SPOTS, 8, 128), F32),
            vmem((NZ, 8, 128), F32),
            vmem((F, NZ * SPOTS, ROWS), F32),
            vmem((8, 128), F32),
            vmem((SPOTS, 8, 128), F32),
            vmem((8, 128), F32),
            vmem((NZ, 8, 128), F32),
            vmem((STRUCTS + 8, 128), F32),
            vmem((F - 1, STRUCTS + 8, 128), F32),
            *pairs_of((F - 1, CHUNKS)),
            *pairs_of((F - 1, F - 1)),
            *pairs_of((NZ, CHUNKS)),
            *pairs_of((3, SPOTS)),
            *pairs_of((NZ,)),
            *pairs_of((NZ, SPOTS)),
            *pairs_of((SPOTS,)),
            *pairs_of((NZ,)),
            *pairs_of((F - 1,)),
        ],
        compiler_params=pltpu.CompilerParams(
            collective_id=0, has_side_effects=True, vmem_limit_bytes=40 * 1024 * 1024),
    )(descriptors, atom_counts, partner_requests, pair_local, pair_slot)


def solution(mesh):
    in_specs = (P("struct", "feat"), P("struct", None), P("struct"), P("struct"), P("struct"))
    out_specs = P(("struct", "feat"))
    return jax.shard_map(
        per_device, mesh=mesh, in_specs=in_specs, out_specs=out_specs, check_vma=False)
```

```python
import jax
import jax.numpy as jnp
from jax import lax
from jax.experimental import pallas as pl
from jax.experimental.pallas import tpu as pltpu
from jax.sharding import PartitionSpec as P

MAXAT = 128
ATOMS_DEV = 1536
STRUCTS = 32
F = 4
NY, NZ, NC = 4, 8, 2
FEATS = 128
DEPTH = F * FEATS
ROWS = ATOMS_DEV // F
TILE = MAXAT // F
SPOTS = NY * NC
WIDE = 512
PAIRS = 384
MESH = pl.DeviceIdType.MESH
BF16, F32 = jnp.bfloat16, jnp.float32

NEAR = [(dy, dc) for dy in range(NY) for dc in range(NC)]
PLANES = (0, 1, 7, 2, 6, 3, 5, 4)
EARLY = 5
BLOCKS = (0, 1, 3, 2)
NT = (((1,), (1,)), ((), ()))


def iota(shape, dim):
    return lax.broadcasted_iota(jnp.int32, shape, dim)


def fiota(shape, dim):
    return iota(shape, dim).astype(F32)


def dot(a, b):
    return jnp.dot(a, b, preferred_element_type=F32)


def split3(x):
    high = x.astype(BF16)
    rest = x - high.astype(F32)
    middle = rest.astype(BF16)
    return high, middle, (rest - middle.astype(F32)).astype(BF16)


def kernel(x_hbm, counts_hbm, req_hbm, local_hbm, slot_hbm, out_ref,
           x_ref, counts_ref, req_ref, local_ref, slot_ref,
           rows, ring, stage, recv, picks, info, asked, sizes, sums, inside, own_self, near_self,
           plane_self, far_self, table, tables,
           in_sem, x_send, x_recv, z_send, z_recv, a_send, a_recv, c_send, c_recv,
           y_send, y_recv, s_send, s_recv, p_send, p_recv, t_send, t_recv):
    s = lax.axis_index("struct")
    f = lax.axis_index("feat")
    y, z, c = s // (NZ * NC), lax.rem(s // NC, NZ), lax.rem(s, NC)
    ff = f.astype(F32)

    def struct_at(dz, dy, dc):
        return (lax.rem(y + dy + NY, NY) * NZ + lax.rem(z + dz + NZ, NZ)) * NC + lax.rem(c + dc, NC)

    def at(dz, dy, dc):
        return {"struct": struct_at(dz, dy, dc)}

    def feat_at(d):
        return {"feat": lax.rem(f + d, F)}

    def copy(src, dst, send, recv_sem, to):
        made = pltpu.make_async_remote_copy(
            src_ref=src, dst_ref=dst, send_sem=send, recv_sem=recv_sem, device_id=to,
            device_id_type=MESH)
        made.start()

    def await_all(like, sem):
        pltpu.make_async_copy(like, like, sem).wait()

    loads = []
    for n, (src, dst) in enumerate(((x_hbm, x_ref), (counts_hbm, counts_ref), (req_hbm, req_ref),
                                    (local_hbm, local_ref), (slot_hbm, slot_ref))):
        loads.append(pltpu.make_async_copy(src, dst, in_sem.at[n]))
        loads[-1].start()

    peers = [at(0, dy, dc) for dy, dc in NEAR[1:]] + [at(1, 0, 0), at(-1, 0, 0)]
    peers += [feat_at(d) for d in range(1, F)]
    barrier = pltpu.get_barrier_semaphore()
    for peer in peers:
        pl.semaphore_signal(barrier, inc=1, device_id=peer, device_id_type=MESH)

    step = 2 * FEATS
    part = step // F
    r, q = iota((step, step), 0), iota((step, step), 1)
    wanted = F * lax.rem(r, part) + lax.rem(r // part + f, F)
    deal = jnp.where(q == wanted, 1.0, 0.0).astype(BF16)
    loads[0].wait()
    for b in range(ATOMS_DEV // step):
        dealt = dot(deal, x_ref[b * step:(b + 1) * step, :]).astype(BF16)
        for e in range(F):
            rows[e * ROWS + b * part:e * ROWS + (b + 1) * part, 0:FEATS] = dealt[e * part:(e + 1) * part, :]

    for load in loads[1:]:
        load.wait()
    counts_row = jnp.concatenate(
        [counts_ref[...].astype(F32), jnp.zeros((1, 128 - STRUCTS), F32)], axis=1)
    req_row = jnp.concatenate(
        [req_ref[...].reshape(1, NY * NZ * NC).astype(F32), jnp.zeros((1, 64), F32)], axis=1)
    sub, lane = iota((STRUCTS, 128), 0), iota((STRUCTS, 128), 1)
    counts_col = jnp.sum(jnp.where(sub == lane, counts_row, 0.0), axis=1, keepdims=True)
    starts_row = jnp.sum(jnp.where(sub < lane, counts_col, 0.0), axis=0, keepdims=True)
    starts_col = jnp.sum(jnp.where(lane < sub, counts_row, 0.0), axis=1, keepdims=True)
    info[...] = jnp.concatenate(
        [req_row, counts_row, starts_row, jnp.zeros((5, 128), F32)], axis=0)
    sizes[0] = info[...]

    pl.semaphore_wait(barrier, len(peers))

    def columns(j):
        return pl.ds(pl.multiple_of(j * FEATS, FEATS), FEATS)

    def hop(o, to, j):
        dst = lax.rem(o + to + NZ, NZ)
        copy(ring.at[o, :, columns(j)], ring.at[dst, :, columns(j)], z_send, z_recv.at[dst, j], at(to, 0, 0))

    def hop_sizes(o, to):
        dst = lax.rem(o + to + NZ, NZ)
        copy(sizes.at[o], sizes.at[dst], c_send, c_recv.at[dst], at(to, 0, 0))

    def move(d, e):
        copy(rows.at[pl.ds((e + d) % F * ROWS, ROWS), pl.ds(0, FEATS)],
             rows.at[pl.ds(e * ROWS, ROWS), pl.ds((F - d) * FEATS, FEATS)],
             x_send, x_recv.at[F - d if e == 0 else 0], feat_at(d))

    def ask(dz, spots):
        for t in spots:
            dy, dc = NEAR[t]
            copy(info, asked.at[dz % 3 * SPOTS + t], a_send, a_recv.at[dz % 3], at(-dz, -dy, dc))

    def enter(j):
        ring[0, :, columns(j)] = rows[0:ROWS, columns(j)]
        hop(0, 1, j)
        hop(0, -1, j)

    enter(0)
    hop_sizes(0, 1)
    hop_sizes(0, -1)
    move(F - 1, 0)
    move(1, 0)
    ask(0, range(1, SPOTS))

    for j in BLOCKS[1:]:
        await_all(rows.at[pl.ds(0, ROWS), columns(j)], x_recv.at[j])
        enter(j)
        if j == BLOCKS[1]:
            move(2, 0)
        if j == BLOCKS[2]:
            for e in range(1, F):
                for d in (F - 1, 1, 2):
                    move(d, e)

    def pick(o, asks_rows):
        n = asks_rows.shape[0]
        sizes_ref = sizes.at[o]
        lanes = iota((n, 128), 1)
        asked_for = jnp.sum(jnp.where(lanes == struct_at(-o, 0, 0), asks_rows, 0.0), axis=1, keepdims=True)
        chosen = lanes.astype(F32) == asked_for
        count = jnp.sum(jnp.where(chosen, sizes_ref[1:2, :], 0.0), axis=1, keepdims=True)
        start = jnp.sum(jnp.where(chosen, sizes_ref[2:3, :], 0.0), axis=1, keepdims=True)
        begin = jnp.floor((start - ff + 3.0) * 0.25)
        end = jnp.floor((start + count - ff + 3.0) * 0.25)
        begin = jnp.broadcast_to(begin, (n, ROWS))
        end = jnp.broadcast_to(end, (n, ROWS))
        i, k = fiota((TILE, ROWS), 0), fiota((TILE, ROWS), 1)
        for t in range(n):
            chosen = (begin[t:t + 1] + i == k) & (k < end[t:t + 1])
            yield jnp.where(chosen, 1.0, 0.0).astype(BF16)

    def tile(n, t, j, to):
        part_rows = pl.ds(t * TILE, TILE)
        stage_rows = pl.ds(pl.multiple_of((n * SPOTS + t) * TILE, TILE), TILE)
        copy(stage.at[stage_rows, columns(j)], recv.at[n, part_rows, columns(j)], y_send, y_recv.at[n], to)

    def serve(o, n, j):
        made = dot(picks[o, 0:SPOTS * TILE], ring[o, :, columns(j)]).astype(BF16)
        stage[pl.ds(pl.multiple_of(n * SPOTS * TILE, TILE), SPOTS * TILE), columns(j)] = made
        recv[n, 0:TILE, columns(j)] = made[0:TILE]
        for t in range(1, SPOTS):
            tile(n, t, j, at(0, *NEAR[t]))

    def serve_far(o, down, j):
        made = dot(picks[o, SPOTS * TILE:], ring[o, :, columns(j)]).astype(BF16)
        for m in range(SPOTS // 2):
            t = 2 * m + down
            at_row = pl.multiple_of(t * TILE, TILE)
            n = NZ - 1
            stage_rows = pl.ds(pl.multiple_of(n * SPOTS * TILE + at_row, TILE), TILE)
            stage[stage_rows, columns(j)] = made[m * TILE:(m + 1) * TILE]
            copy(stage.at[stage_rows, columns(j)], recv.at[n, pl.ds(at_row, TILE), columns(j)],
                 y_send, y_recv.at[n], at(1 - 2 * down, m, down))

    def products(n):
        for b in range(ATOMS_DEV // WIDE):
            cols = slice(b * WIDE, (b + 1) * WIDE)
            p = lax.dot_general(recv[n], rows[cols, :], NT, preferred_element_type=F32)
            sums[pl.ds(pl.multiple_of(n * SPOTS, SPOTS), SPOTS), cols] = jnp.sum(
                (p * p).reshape(SPOTS, TILE, WIDE), axis=1)

    def near_products(n, carry):
        await_all(recv.at[n, pl.ds(TILE, (SPOTS - 1) * TILE)], y_recv.at[n])
        products(n)
        return carry

    def by_structure(first, last):
        return sum(
            lax.dot_general(inside[...], piece, NT, preferred_element_type=F32)
            for piece in split3(sums[first * SPOTS:last * SPOTS]))

    await_all(asked.at[pl.ds(0, SPOTS - 1)], a_recv.at[0])
    near_asks = jnp.concatenate([info[0:1, :]] + [asked[t, 0:1, :] for t in range(1, SPOTS)], axis=0)

    def pick_near(o):
        for t, chosen in enumerate(pick(o, near_asks)):
            picks[o, t * TILE:(t + 1) * TILE] = chosen

    pick_near(0)

    def own_block(j, carry):
        serve(0, 0, j)
        return carry

    lax.fori_loop(0, F, own_block, 0)

    def block_at(m):
        return jnp.where(m < 2, m, F + 1 - m)

    def next_hop(i, carry):
        hop_no, m = i // F + 1, lax.rem(i, F)
        j = block_at(m)

        def arrive(down, carry):
            o = jnp.where(down == 0, hop_no, NZ - hop_no)
            await_all(ring.at[o, :, columns(j)], z_recv.at[o, j])
            hop(o, 1 - 2 * down, j)

            @pl.when(m == 0)
            def _():
                await_all(sizes.at[o], c_recv.at[o])
                hop_sizes(o, 1 - 2 * down)
            return carry

        lax.fori_loop(0, 2, arrive, 0)

        @pl.when(i == 0)
        def _():
            ask(1, range(0, SPOTS, 2))
            ask(-1, range(1, SPOTS, 2))

        def send(down, carry):
            o = jnp.where(down == 0, hop_no, NZ - hop_no)

            @pl.when(m == 0)
            def _():
                pick_near(o)

            serve(o, 2 * hop_no - 1 + down, j)
            return carry

        lax.fori_loop(0, 2, send, 0)
        return carry

    lax.fori_loop(0, 2 * F, next_hop, 0)

    column = iota((STRUCTS, ATOMS_DEV), 1)
    e_of = sum(jnp.where(column >= n * ROWS, 1, 0) for n in range(1, F))
    index = F * (column - ROWS * e_of) + lax.rem(f + e_of, F)
    index = index.astype(F32)
    belongs = (starts_col <= index) & (index < starts_col + counts_col)
    inside[...] = jnp.where(belongs, 1.0, 0.0).astype(BF16)
    seg_row = jnp.sum(jnp.where(belongs, fiota((STRUCTS, ATOMS_DEV), 0), 0.0), axis=0, keepdims=True)
    own_row = F * fiota((ROWS, 128), 0) + ff
    own_seg = jnp.sum(
        jnp.where((starts_row + counts_row <= own_row) & (iota((ROWS, 128), 1) < STRUCTS), 1.0, 0.0),
        axis=1, keepdims=True)

    def self_kernel():
        total = jnp.zeros((STRUCTS, 1), F32)
        for b in range(ATOMS_DEV // WIDE):
            cols = slice(b * WIDE, (b + 1) * WIDE)
            p = lax.dot_general(rows[0:ROWS, :], rows[cols, :], NT, preferred_element_type=F32)
            p = jnp.where(own_seg == seg_row[:, cols], p, 0.0)
            by_column = jnp.sum(p * p, axis=0, keepdims=True)
            total = total + jnp.sum(
                jnp.where(inside[:, cols].astype(F32) > 0.5, by_column, 0.0), axis=1, keepdims=True)
        return total

    await_all(rows.at[pl.ds(ROWS, (F - 1) * ROWS), pl.ds(FEATS, (F - 1) * FEATS)], x_recv.at[0])
    self_col = self_kernel()
    own_self[...] = jnp.broadcast_to(
        jnp.sum(jnp.where(sub == lane, self_col, 0.0), axis=0, keepdims=True), (8, 128))
    for t in range(1, SPOTS):
        copy(own_self, near_self.at[t], s_send, s_recv, at(0, *NEAR[t]))

    def spread_self():
        await_all(near_self.at[pl.ds(1, SPOTS - 1)], s_recv)
        plane_self[...] = jnp.concatenate(
            [own_self[0:1, :]] + [near_self[t, 0:1, :] for t in range(1, SPOTS)], axis=0)
        for o in range(1, NZ):
            copy(plane_self, far_self.at[o], p_send, p_recv, at(o, 0, 0))

    def last_hop(m, carry):
        j = block_at(m)

        def send(down, carry):
            o = jnp.where(down == 0, 3, NZ - 3)
            await_all(ring.at[o, :, columns(j)], z_recv.at[o, j])

            @pl.when(m == 0)
            def _():
                await_all(sizes.at[o], c_recv.at[o])
                pick_near(o)
                await_all(asked.at[pl.ds(0, SPOTS // 2)], a_recv.at[1 + down])
                far_asks = jnp.concatenate(
                    [asked[(1 + down) * SPOTS + 2 * t + down, 0:1, :] for t in range(SPOTS // 2)], axis=0)
                for t, chosen in enumerate(pick(o, far_asks)):
                    picks[o, (SPOTS + t) * TILE:(SPOTS + t + 1) * TILE] = chosen

            serve_far(o, down, j)
            serve(o, 5 + down, j)
            return carry

        lax.fori_loop(0, 2, send, 0)

        @pl.when(m == 1)
        def _():
            spread_self()

        return carry

    lax.fori_loop(0, F, last_hop, 0)

    lax.fori_loop(0, EARLY, near_products, 0)
    early = by_structure(0, EARLY)

    def holder_of(spot):
        n = spot // SPOTS
        t = lax.rem(spot, SPOTS)
        o = sum(jnp.where(n == m, plane, 0) for m, plane in enumerate(PLANES))
        return (lax.rem(y - t // NC + NY, NY) * NZ + lax.rem(z - o + NZ, NZ)) * NC + lax.rem(
            c + lax.rem(t, NC), NC)

    holders = NZ * SPOTS
    spot, lanes = iota((holders, 128), 0), iota((holders, 128), 1)
    my_request = jnp.sum(jnp.where(lanes == holder_of(spot), info[0:1, :], 0.0), axis=1, keepdims=True)
    await_all(far_self.at[pl.ds(1, NZ - 1)], p_recv)
    all_self = jnp.concatenate([far_self[o] if o else plane_self[...] for o in PLANES], axis=0)
    partner_self = jnp.sum(jnp.where(lanes.astype(F32) == my_request, all_self, 0.0), axis=1, keepdims=True)
    partner_row = jnp.sum(jnp.where(lanes == spot, partner_self, 0.0), axis=0, keepdims=True)
    table[STRUCTS:STRUCTS + 8, :] = jnp.broadcast_to(partner_row, (8, 128))

    pairs = pl.ds(pl.multiple_of(f * PAIRS, 128), PAIRS)
    spot = iota((128, PAIRS), 0)
    slot_pick = jnp.where(
        (holder_of(spot) == slot_ref[pairs].reshape(1, PAIRS)) & (spot < holders), 1.0, 0.0).astype(BF16)
    local_pick = iota((STRUCTS, PAIRS), 0) == local_ref[pairs].reshape(1, PAIRS)

    lax.fori_loop(EARLY, NZ - 1, near_products, 0)
    await_all(recv.at[NZ - 1], y_recv.at[NZ - 1])
    products(NZ - 1)
    late = by_structure(EARLY, NZ)
    table[0:STRUCTS, :] = jnp.concatenate(
        [early, late, jnp.broadcast_to(self_col, (STRUCTS, 128 - holders))], axis=1)
    for d in range(1, F):
        copy(table, tables.at[d - 1], t_send, t_recv, feat_at(d))
    await_all(rows.at[:, pl.ds(FEATS, (F - 1) * FEATS)], x_send)
    await_all(ring.at[pl.ds(0, 6)], z_send)
    await_all(sizes.at[pl.ds(0, 6)], c_send)
    await_all(asked.at[pl.ds(0, 2 * SPOTS - 1)], a_send)
    await_all(stage.at[pl.ds(0, ((NZ - 1) * (SPOTS - 1) + SPOTS) * TILE)], y_send)
    await_all(near_self.at[pl.ds(0, SPOTS - 1)], s_send)
    await_all(far_self.at[pl.ds(0, NZ - 1)], p_send)
    await_all(tables, t_recv)
    await_all(tables, t_send)
    total = (table[...] + tables[0]) + (tables[1] + tables[2])
    picked = sum(dot(piece, slot_pick) for piece in split3(total))
    left_self = jnp.sum(jnp.where(local_pick, total[0:STRUCTS, holders:holders + 1], 0.0), axis=0, keepdims=True)
    value = jnp.sum(jnp.where(local_pick, picked[0:STRUCTS], 0.0), axis=0, keepdims=True)
    right_self = picked[STRUCTS:STRUCTS + 1]
    out_ref[...] = (value / jnp.sqrt(left_self * right_self)).reshape(PAIRS)


def per_device(descriptors, atom_counts, partner_requests, pair_local, pair_slot):
    dma = pltpu.SemaphoreType.DMA
    vmem = pltpu.VMEM

    inputs = (descriptors, atom_counts, partner_requests, pair_local, pair_slot)
    return pl.pallas_call(
        kernel,
        out_shape=jax.ShapeDtypeStruct((PAIRS,), F32),
        in_specs=[pl.BlockSpec(memory_space=pl.ANY)] * 5,
        out_specs=pl.BlockSpec(memory_space=vmem),
        scratch_shapes=[
            *[vmem(a.shape, a.dtype) for a in inputs],
            vmem((ATOMS_DEV, DEPTH), BF16),
            vmem((NZ, ROWS, DEPTH), BF16),
            vmem((NZ * SPOTS * TILE, DEPTH), BF16),
            vmem((NZ, SPOTS * TILE, DEPTH), BF16),
            vmem((NZ, (SPOTS + SPOTS // 2) * TILE, ROWS), BF16),
            vmem((8, 128), F32),
            vmem((3 * SPOTS, 8, 128), F32),
            vmem((NZ, 8, 128), F32),
            vmem((NZ * SPOTS, ATOMS_DEV), F32),
            vmem((STRUCTS, ATOMS_DEV), BF16),
            vmem((8, 128), F32),
            vmem((SPOTS, 8, 128), F32),
            vmem((8, 128), F32),
            vmem((NZ, 8, 128), F32),
            vmem((STRUCTS + 8, 128), F32),
            vmem((F - 1, STRUCTS + 8, 128), F32),
            dma((5,)),
            dma(()), dma((F,)),
            dma(()), dma((NZ, F)),
            dma(()), dma((3,)),
            dma(()), dma((NZ,)),
            dma(()), dma((NZ,)),
            dma(()), dma(()),
            dma(()), dma(()),
            dma(()), dma(()),
        ],
        compiler_params=pltpu.CompilerParams(
            collective_id=0, has_side_effects=True, vmem_limit_bytes=62 * 1024 * 1024),
    )(*inputs)


def solution(mesh):
    in_specs = (P("struct", "feat"), P("struct", None), P("struct"), P("struct"), P("struct"))
    out_specs = P(("struct", "feat"))
    return jax.shard_map(
        per_device, mesh=mesh, in_specs=in_specs, out_specs=out_specs, check_vma=False)
```

```python
import jax
import jax.numpy as jnp
from jax import lax
from jax.experimental import pallas as pl
from jax.experimental.pallas import tpu as pltpu
from jax.sharding import PartitionSpec as P

MAXAT = 128
ATOMS_DEV = 1536
STRUCTS = 32
F = 4
NY, NZ, NC = 4, 8, 2
FEATS = 128
DEPTH = F * FEATS
ROWS = ATOMS_DEV // F
TILE = MAXAT // F
SPOTS = NY * NC
WIDE = 512
PAIRS = 384
MESH = pl.DeviceIdType.MESH
BF16, F32 = jnp.bfloat16, jnp.float32

NEAR = [(dy, dc) for dy in range(NY) for dc in range(NC)]
PLANES = (0, 1, 7, 2, 6, 3, 5, 4)
EARLY = 5
BLOCKS = (0, 1, 3, 2)
NT = (((1,), (1,)), ((), ()))


def iota(shape, dim):
    return lax.broadcasted_iota(jnp.int32, shape, dim)


def fiota(shape, dim):
    return iota(shape, dim).astype(F32)


def dot(a, b):
    return jnp.dot(a, b, preferred_element_type=F32)


def split3(x):
    high = x.astype(BF16)
    rest = x - high.astype(F32)
    middle = rest.astype(BF16)
    return high, middle, (rest - middle.astype(F32)).astype(BF16)


def kernel(x_hbm, counts_hbm, req_hbm, local_hbm, slot_hbm, out_ref,
           x_ref, counts_ref, req_ref, local_ref, slot_ref,
           rows, ring, stage, recv, picks, info, asked, sizes, sums, inside, own_self, near_self,
           plane_self, far_self, table, tables,
           in_sem, xh_recv, x_send, x_recv, z_send, z_recv, a_send, a_recv, c_send, c_recv,
           y_send, y_recv, s_send, s_recv, p_send, p_recv, t_send, t_recv):
    s = lax.axis_index("struct")
    f = lax.axis_index("feat")
    y, z, c = s // (NZ * NC), lax.rem(s // NC, NZ), lax.rem(s, NC)
    ff = f.astype(F32)

    def struct_at(dz, dy, dc):
        return (lax.rem(y + dy + NY, NY) * NZ + lax.rem(z + dz + NZ, NZ)) * NC + lax.rem(c + dc, NC)

    def at(dz, dy, dc):
        return {"struct": struct_at(dz, dy, dc)}

    def feat_at(d):
        return {"feat": lax.rem(f + d, F)}

    def copy(src, dst, send, recv_sem, to):
        made = pltpu.make_async_remote_copy(
            src_ref=src, dst_ref=dst, send_sem=send, recv_sem=recv_sem, device_id=to,
            device_id_type=MESH)
        made.start()

    def await_all(like, sem):
        pltpu.make_async_copy(like, like, sem).wait()

    loads = []
    for n, (src, dst) in enumerate(((x_hbm, x_ref), (counts_hbm, counts_ref), (req_hbm, req_ref),
                                    (local_hbm, local_ref), (slot_hbm, slot_ref))):
        loads.append(pltpu.make_async_copy(src, dst, in_sem.at[n]))
        loads[-1].start()

    peers = [at(0, dy, dc) for dy, dc in NEAR[1:]] + [at(1, 0, 0), at(-1, 0, 0)]
    peers += [feat_at(d) for d in range(1, F)]
    barrier = pltpu.get_barrier_semaphore()
    for peer in peers:
        pl.semaphore_signal(barrier, inc=1, device_id=peer, device_id_type=MESH)

    step = 2 * FEATS
    part = step // F
    r, q = iota((step, step), 0), iota((step, step), 1)
    wanted = F * lax.rem(r, part) + lax.rem(r // part + f, F)
    deal = jnp.where(q == wanted, 1.0, 0.0).astype(BF16)
    loads[0].wait()
    for b in range(ATOMS_DEV // step):
        dealt = dot(deal, x_ref[b * step:(b + 1) * step, :]).astype(BF16)
        for e in range(F):
            rows[e * ROWS + b * part:e * ROWS + (b + 1) * part, 0:FEATS] = dealt[e * part:(e + 1) * part, :]

    for load in loads[1:]:
        load.wait()
    counts_row = jnp.concatenate(
        [counts_ref[...].astype(F32), jnp.zeros((1, 128 - STRUCTS), F32)], axis=1)
    req_row = jnp.concatenate(
        [req_ref[...].reshape(1, NY * NZ * NC).astype(F32), jnp.zeros((1, 64), F32)], axis=1)
    sub, lane = iota((STRUCTS, 128), 0), iota((STRUCTS, 128), 1)
    counts_col = jnp.sum(jnp.where(sub == lane, counts_row, 0.0), axis=1, keepdims=True)
    starts_row = jnp.sum(jnp.where(sub < lane, counts_col, 0.0), axis=0, keepdims=True)
    starts_col = jnp.sum(jnp.where(lane < sub, counts_row, 0.0), axis=1, keepdims=True)
    info[...] = jnp.concatenate(
        [req_row, counts_row, starts_row, jnp.zeros((5, 128), F32)], axis=0)
    sizes[0] = info[...]

    pl.semaphore_wait(barrier, len(peers))

    def columns(j):
        return pl.ds(pl.multiple_of(j * FEATS, FEATS), FEATS)

    def hop(o, to, j):
        dst = lax.rem(o + to + NZ, NZ)
        copy(ring.at[o, :, columns(j)], ring.at[dst, :, columns(j)], z_send, z_recv.at[dst, j], at(to, 0, 0))

    def hop_sizes(o, to):
        dst = lax.rem(o + to + NZ, NZ)
        copy(sizes.at[o], sizes.at[dst], c_send, c_recv.at[dst], at(to, 0, 0))

    def move(d, e):
        copy(rows.at[pl.ds((e + d) % F * ROWS, ROWS), pl.ds(0, FEATS)],
             rows.at[pl.ds(e * ROWS, ROWS), pl.ds((F - d) * FEATS, FEATS)],
             x_send, x_recv.at[F - d if e == 0 else 0], feat_at(d))

    def halves(half):
        return pl.ds(half * ROWS // 4, ROWS // 4)

    def move_half(d, half):
        copy(rows.at[pl.ds(d * ROWS + half * ROWS // 4, ROWS // 4), pl.ds(0, FEATS)],
             rows.at[halves(half), pl.ds((F - d) * FEATS, FEATS)],
             x_send, xh_recv.at[F - d, half], feat_at(d))

    def enter_half(j, half):
        ring[0, halves(half), columns(j)] = rows[halves(half), columns(j)]
        for to in (1, NZ - 1):
            copy(ring.at[0, halves(half), columns(j)], ring.at[to, halves(half), columns(j)],
                 z_send, z_recv.at[to, j], at(1 if to == 1 else -1, 0, 0))

    def ask(dz, spots):
        for t in spots:
            dy, dc = NEAR[t]
            copy(info, asked.at[dz % 3 * SPOTS + t], a_send, a_recv.at[dz % 3], at(-dz, -dy, dc))

    def enter(j):
        ring[0, :, columns(j)] = rows[0:ROWS, columns(j)]
        hop(0, 1, j)
        hop(0, -1, j)

    enter(0)
    hop_sizes(0, 1)
    hop_sizes(0, -1)
    for half in range(4):
        move_half(F - 1, half)
        move_half(1, half)
    move(2, 0)
    ask(0, range(1, SPOTS))

    for j in BLOCKS[1:]:
        if j == 2:
            await_all(rows.at[pl.ds(0, ROWS), columns(j)], x_recv.at[j])
            enter(j)
        else:
            for half in range(4):
                await_all(rows.at[halves(half), columns(j)], xh_recv.at[j, half])
                enter_half(j, half)
        if j == BLOCKS[2]:
            for e in range(1, F):
                for d in (F - 1, 1, 2):
                    move(d, e)

    def pick(o, asks_rows):
        n = asks_rows.shape[0]
        sizes_ref = sizes.at[o]
        lanes = iota((n, 128), 1)
        asked_for = jnp.sum(jnp.where(lanes == struct_at(-o, 0, 0), asks_rows, 0.0), axis=1, keepdims=True)
        chosen = lanes.astype(F32) == asked_for
        count = jnp.sum(jnp.where(chosen, sizes_ref[1:2, :], 0.0), axis=1, keepdims=True)
        start = jnp.sum(jnp.where(chosen, sizes_ref[2:3, :], 0.0), axis=1, keepdims=True)
        begin = jnp.floor((start - ff + 3.0) * 0.25)
        end = jnp.floor((start + count - ff + 3.0) * 0.25)
        begin = jnp.broadcast_to(begin, (n, ROWS))
        end = jnp.broadcast_to(end, (n, ROWS))
        i, k = fiota((TILE, ROWS), 0), fiota((TILE, ROWS), 1)
        for t in range(n):
            chosen = (begin[t:t + 1] + i == k) & (k < end[t:t + 1])
            yield jnp.where(chosen, 1.0, 0.0).astype(BF16)

    def tile(n, t, j, to):
        part_rows = pl.ds(t * TILE, TILE)
        stage_rows = pl.ds(pl.multiple_of((n * SPOTS + t) * TILE, TILE), TILE)
        copy(stage.at[stage_rows, columns(j)], recv.at[n, part_rows, columns(j)], y_send, y_recv.at[n], to)

    def serve(o, n, j):
        made = dot(picks[o, 0:SPOTS * TILE], ring[o, :, columns(j)]).astype(BF16)
        stage[pl.ds(pl.multiple_of(n * SPOTS * TILE, TILE), SPOTS * TILE), columns(j)] = made
        recv[n, 0:TILE, columns(j)] = made[0:TILE]
        for t in range(1, SPOTS):
            tile(n, t, j, at(0, *NEAR[t]))

    def serve_far(o, down, j):
        made = dot(picks[o, SPOTS * TILE:], ring[o, :, columns(j)]).astype(BF16)
        for m in range(SPOTS // 2):
            t = 2 * m + down
            at_row = pl.multiple_of(t * TILE, TILE)
            n = NZ - 1
            stage_rows = pl.ds(pl.multiple_of(n * SPOTS * TILE + at_row, TILE), TILE)
            stage[stage_rows, columns(j)] = made[m * TILE:(m + 1) * TILE]
            copy(stage.at[stage_rows, columns(j)], recv.at[n, pl.ds(at_row, TILE), columns(j)],
                 y_send, y_recv.at[n], at(1 - 2 * down, m, down))

    def products(n):
        for b in range(ATOMS_DEV // WIDE):
            cols = slice(b * WIDE, (b + 1) * WIDE)
            p = lax.dot_general(recv[n], rows[cols, :], NT, preferred_element_type=F32)
            sums[pl.ds(pl.multiple_of(n * SPOTS, SPOTS), SPOTS), cols] = jnp.sum(
                (p * p).reshape(SPOTS, TILE, WIDE), axis=1)

    def near_products(n, carry):
        await_all(recv.at[n, pl.ds(TILE, (SPOTS - 1) * TILE)], y_recv.at[n])
        products(n)
        return carry

    def by_structure(first, last):
        return sum(
            lax.dot_general(inside[...], piece, NT, preferred_element_type=F32)
            for piece in split3(sums[first * SPOTS:last * SPOTS]))

    await_all(asked.at[pl.ds(0, SPOTS - 1)], a_recv.at[0])
    near_asks = jnp.concatenate([info[0:1, :]] + [asked[t, 0:1, :] for t in range(1, SPOTS)], axis=0)

    def pick_near(o):
        for t, chosen in enumerate(pick(o, near_asks)):
            picks[o, t * TILE:(t + 1) * TILE] = chosen

    pick_near(0)

    def own_block(j, carry):
        serve(0, 0, j)
        return carry

    lax.fori_loop(0, F, own_block, 0)

    def block_at(m):
        return jnp.where(m < 2, m, F + 1 - m)

    def next_hop(i, carry):
        hop_no, m = i // F + 1, lax.rem(i, F)
        j = block_at(m)

        def arrive(down, carry):
            o = jnp.where(down == 0, hop_no, NZ - hop_no)
            await_all(ring.at[o, :, columns(j)], z_recv.at[o, j])
            hop(o, 1 - 2 * down, j)

            @pl.when(m == 0)
            def _():
                await_all(sizes.at[o], c_recv.at[o])
                hop_sizes(o, 1 - 2 * down)
            return carry

        lax.fori_loop(0, 2, arrive, 0)

        @pl.when(i == 0)
        def _():
            ask(1, range(0, SPOTS, 2))
            ask(-1, range(1, SPOTS, 2))

        def send(down, carry):
            o = jnp.where(down == 0, hop_no, NZ - hop_no)

            @pl.when(m == 0)
            def _():
                pick_near(o)

            serve(o, 2 * hop_no - 1 + down, j)
            return carry

        lax.fori_loop(0, 2, send, 0)
        return carry

    lax.fori_loop(0, 2 * F, next_hop, 0)

    column = iota((STRUCTS, ATOMS_DEV), 1)
    e_of = sum(jnp.where(column >= n * ROWS, 1, 0) for n in range(1, F))
    index = F * (column - ROWS * e_of) + lax.rem(f + e_of, F)
    index = index.astype(F32)
    belongs = (starts_col <= index) & (index < starts_col + counts_col)
    inside[...] = jnp.where(belongs, 1.0, 0.0).astype(BF16)
    seg_row = jnp.sum(jnp.where(belongs, fiota((STRUCTS, ATOMS_DEV), 0), 0.0), axis=0, keepdims=True)
    own_row = F * fiota((ROWS, 128), 0) + ff
    own_seg = jnp.sum(
        jnp.where((starts_row + counts_row <= own_row) & (iota((ROWS, 128), 1) < STRUCTS), 1.0, 0.0),
        axis=1, keepdims=True)

    def self_kernel():
        total = jnp.zeros((STRUCTS, 1), F32)
        for b in range(ATOMS_DEV // WIDE):
            cols = slice(b * WIDE, (b + 1) * WIDE)
            p = lax.dot_general(rows[0:ROWS, :], rows[cols, :], NT, preferred_element_type=F32)
            p = jnp.where(own_seg == seg_row[:, cols], p, 0.0)
            by_column = jnp.sum(p * p, axis=0, keepdims=True)
            total = total + jnp.sum(
                jnp.where(inside[:, cols].astype(F32) > 0.5, by_column, 0.0), axis=1, keepdims=True)
        return total

    await_all(rows.at[pl.ds(ROWS, (F - 1) * ROWS), pl.ds(FEATS, (F - 1) * FEATS)], x_recv.at[0])
    self_col = self_kernel()
    own_self[...] = jnp.broadcast_to(
        jnp.sum(jnp.where(sub == lane, self_col, 0.0), axis=0, keepdims=True), (8, 128))
    for t in range(1, SPOTS):
        copy(own_self, near_self.at[t], s_send, s_recv, at(0, *NEAR[t]))

    def spread_self():
        await_all(near_self.at[pl.ds(1, SPOTS - 1)], s_recv)
        plane_self[...] = jnp.concatenate(
            [own_self[0:1, :]] + [near_self[t, 0:1, :] for t in range(1, SPOTS)], axis=0)
        for o in range(1, NZ):
            copy(plane_self, far_self.at[o], p_send, p_recv, at(o, 0, 0))

    def last_hop(m, carry):
        j = block_at(m)

        def send(down, carry):
            o = jnp.where(down == 0, 3, NZ - 3)
            await_all(ring.at[o, :, columns(j)], z_recv.at[o, j])

            @pl.when(m == 0)
            def _():
                await_all(sizes.at[o], c_recv.at[o])
                pick_near(o)
                await_all(asked.at[pl.ds(0, SPOTS // 2)], a_recv.at[1 + down])
                far_asks = jnp.concatenate(
                    [asked[(1 + down) * SPOTS + 2 * t + down, 0:1, :] for t in range(SPOTS // 2)], axis=0)
                for t, chosen in enumerate(pick(o, far_asks)):
                    picks[o, (SPOTS + t) * TILE:(SPOTS + t + 1) * TILE] = chosen

            serve_far(o, down, j)
            serve(o, 5 + down, j)
            return carry

        lax.fori_loop(0, 2, send, 0)

        @pl.when(m == 3)
        def _():
            spread_self()

        return carry

    lax.fori_loop(0, F, last_hop, 0)

    lax.fori_loop(0, EARLY, near_products, 0)
    early = by_structure(0, EARLY)

    def holder_of(spot):
        n = spot // SPOTS
        t = lax.rem(spot, SPOTS)
        o = sum(jnp.where(n == m, plane, 0) for m, plane in enumerate(PLANES))
        return (lax.rem(y - t // NC + NY, NY) * NZ + lax.rem(z - o + NZ, NZ)) * NC + lax.rem(
            c + lax.rem(t, NC), NC)

    holders = NZ * SPOTS
    spot, lanes = iota((holders, 128), 0), iota((holders, 128), 1)
    my_request = jnp.sum(jnp.where(lanes == holder_of(spot), info[0:1, :], 0.0), axis=1, keepdims=True)
    await_all(far_self.at[pl.ds(1, NZ - 1)], p_recv)
    all_self = jnp.concatenate([far_self[o] if o else plane_self[...] for o in PLANES], axis=0)
    partner_self = jnp.sum(jnp.where(lanes.astype(F32) == my_request, all_self, 0.0), axis=1, keepdims=True)
    partner_row = jnp.sum(jnp.where(lanes == spot, partner_self, 0.0), axis=0, keepdims=True)
    table[STRUCTS:STRUCTS + 8, :] = jnp.broadcast_to(partner_row, (8, 128))

    pairs = pl.ds(pl.multiple_of(f * PAIRS, 128), PAIRS)
    spot = iota((128, PAIRS), 0)
    slot_pick = jnp.where(
        (holder_of(spot) == slot_ref[pairs].reshape(1, PAIRS)) & (spot < holders), 1.0, 0.0).astype(BF16)
    local_pick = iota((STRUCTS, PAIRS), 0) == local_ref[pairs].reshape(1, PAIRS)

    lax.fori_loop(EARLY, NZ - 1, near_products, 0)
    await_all(recv.at[NZ - 1], y_recv.at[NZ - 1])
    products(NZ - 1)
    late = by_structure(EARLY, NZ)
    table[0:STRUCTS, :] = jnp.concatenate(
        [early, late, jnp.broadcast_to(self_col, (STRUCTS, 128 - holders))], axis=1)
    for d in range(1, F):
        copy(table, tables.at[d - 1], t_send, t_recv, feat_at(d))
    await_all(rows.at[:, pl.ds(FEATS, (F - 1) * FEATS)], x_send)
    await_all(ring.at[pl.ds(0, 6)], z_send)
    await_all(sizes.at[pl.ds(0, 6)], c_send)
    await_all(asked.at[pl.ds(0, 2 * SPOTS - 1)], a_send)
    await_all(stage.at[pl.ds(0, ((NZ - 1) * (SPOTS - 1) + SPOTS) * TILE)], y_send)
    await_all(near_self.at[pl.ds(0, SPOTS - 1)], s_send)
    await_all(far_self.at[pl.ds(0, NZ - 1)], p_send)
    await_all(tables, t_recv)
    await_all(tables, t_send)
    total = (table[...] + tables[0]) + (tables[1] + tables[2])
    picked = sum(dot(piece, slot_pick) for piece in split3(total))
    left_self = jnp.sum(jnp.where(local_pick, total[0:STRUCTS, holders:holders + 1], 0.0), axis=0, keepdims=True)
    value = jnp.sum(jnp.where(local_pick, picked[0:STRUCTS], 0.0), axis=0, keepdims=True)
    right_self = picked[STRUCTS:STRUCTS + 1]
    out_ref[...] = (value / jnp.sqrt(left_self * right_self)).reshape(PAIRS)


def per_device(descriptors, atom_counts, partner_requests, pair_local, pair_slot):
    dma = pltpu.SemaphoreType.DMA
    vmem = pltpu.VMEM

    inputs = (descriptors, atom_counts, partner_requests, pair_local, pair_slot)
    return pl.pallas_call(
        kernel,
        out_shape=jax.ShapeDtypeStruct((PAIRS,), F32),
        in_specs=[pl.BlockSpec(memory_space=pl.ANY)] * 5,
        out_specs=pl.BlockSpec(memory_space=vmem),
        scratch_shapes=[
            *[vmem(a.shape, a.dtype) for a in inputs],
            vmem((ATOMS_DEV, DEPTH), BF16),
            vmem((NZ, ROWS, DEPTH), BF16),
            vmem((NZ * SPOTS * TILE, DEPTH), BF16),
            vmem((NZ, SPOTS * TILE, DEPTH), BF16),
            vmem((NZ, (SPOTS + SPOTS // 2) * TILE, ROWS), BF16),
            vmem((8, 128), F32),
            vmem((3 * SPOTS, 8, 128), F32),
            vmem((NZ, 8, 128), F32),
            vmem((NZ * SPOTS, ATOMS_DEV), F32),
            vmem((STRUCTS, ATOMS_DEV), BF16),
            vmem((8, 128), F32),
            vmem((SPOTS, 8, 128), F32),
            vmem((8, 128), F32),
            vmem((NZ, 8, 128), F32),
            vmem((STRUCTS + 8, 128), F32),
            vmem((F - 1, STRUCTS + 8, 128), F32),
            dma((5,)), dma((F, 4)),
            dma(()), dma((F,)),
            dma(()), dma((NZ, F)),
            dma(()), dma((3,)),
            dma(()), dma((NZ,)),
            dma(()), dma((NZ,)),
            dma(()), dma(()),
            dma(()), dma(()),
            dma(()), dma(()),
        ],
        compiler_params=pltpu.CompilerParams(
            collective_id=0, has_side_effects=True, vmem_limit_bytes=62 * 1024 * 1024),
    )(*inputs)


def solution(mesh):
    in_specs = (P("struct", "feat"), P("struct", None), P("struct"), P("struct"), P("struct"))
    out_specs = P(("struct", "feat"))
    return jax.shard_map(
        per_device, mesh=mesh, in_specs=in_specs, out_specs=out_specs, check_vma=False)
```

```python
import jax
import jax.numpy as jnp
from jax import lax
from jax.experimental import pallas as pl
from jax.experimental.pallas import tpu as pltpu
from jax.sharding import PartitionSpec as P

MAXAT = 128
ATOMS_DEV = 1536
STRUCTS = 32
F = 4
NY, NZ, NC = 4, 8, 2
FEATS = 128
DEPTH = F * FEATS
ROWS = ATOMS_DEV // F
TILE = MAXAT // F
SPOTS = NY * NC
WIDE = 512
PAIRS = 384
MESH = pl.DeviceIdType.MESH
BF16, F32 = jnp.bfloat16, jnp.float32

NEAR = [(dy, dc) for dy in range(NY) for dc in range(NC)]
PLANES = (0, 1, 7, 2, 6, 3, 5, 4)
EARLY = 5
BLOCKS = (0, 1, 3, 2)
NT = (((1,), (1,)), ((), ()))


def iota(shape, dim):
    return lax.broadcasted_iota(jnp.int32, shape, dim)


def fiota(shape, dim):
    return iota(shape, dim).astype(F32)


def dot(a, b):
    return jnp.dot(a, b, preferred_element_type=F32)


def split3(x):
    high = x.astype(BF16)
    rest = x - high.astype(F32)
    middle = rest.astype(BF16)
    return high, middle, (rest - middle.astype(F32)).astype(BF16)


def kernel(x_hbm, counts_hbm, req_hbm, local_hbm, slot_hbm, out_ref,
           x_ref, counts_ref, req_ref, local_ref, slot_ref,
           rows, ring, stage, recv, picks, info, asked, sizes, sums, inside, own_self, near_self,
           plane_self, far_self, table, tables,
           in_sem, xh_recv, x_send, x_recv, z_send, z_recv, a_send, a_recv, c_send, c_recv,
           y_send, y_recv, s_send, s_recv, p_send, p_recv, t_send, t_recv):
    s = lax.axis_index("struct")
    f = lax.axis_index("feat")
    y, z, c = s // (NZ * NC), lax.rem(s // NC, NZ), lax.rem(s, NC)
    ff = f.astype(F32)

    def struct_at(dz, dy, dc):
        return (lax.rem(y + dy + NY, NY) * NZ + lax.rem(z + dz + NZ, NZ)) * NC + lax.rem(c + dc, NC)

    def at(dz, dy, dc):
        return {"struct": struct_at(dz, dy, dc)}

    def feat_at(d):
        return {"feat": lax.rem(f + d, F)}

    def copy(src, dst, send, recv_sem, to):
        made = pltpu.make_async_remote_copy(
            src_ref=src, dst_ref=dst, send_sem=send, recv_sem=recv_sem, device_id=to,
            device_id_type=MESH)
        made.start()

    def await_all(like, sem):
        pltpu.make_async_copy(like, like, sem).wait()

    loads = []
    for n, (src, dst) in enumerate(((x_hbm, x_ref), (counts_hbm, counts_ref), (req_hbm, req_ref),
                                    (local_hbm, local_ref), (slot_hbm, slot_ref))):
        loads.append(pltpu.make_async_copy(src, dst, in_sem.at[n]))
        loads[-1].start()

    peers = [at(0, dy, dc) for dy, dc in NEAR[1:]] + [at(1, 0, 0), at(-1, 0, 0)]
    peers += [feat_at(d) for d in range(1, F)]
    barrier = pltpu.get_barrier_semaphore()
    for peer in peers:
        pl.semaphore_signal(barrier, inc=1, device_id=peer, device_id_type=MESH)

    step = 2 * FEATS
    part = step // F
    r, q = iota((step, step), 0), iota((step, step), 1)
    wanted = F * lax.rem(r, part) + lax.rem(r // part + f, F)
    deal = jnp.where(q == wanted, 1.0, 0.0).astype(BF16)
    loads[0].wait()
    for b in range(ATOMS_DEV // step):
        dealt = dot(deal, x_ref[b * step:(b + 1) * step, :]).astype(BF16)
        for e in range(F):
            rows[e * ROWS + b * part:e * ROWS + (b + 1) * part, 0:FEATS] = dealt[e * part:(e + 1) * part, :]

    for load in loads[1:]:
        load.wait()
    counts_row = jnp.concatenate(
        [counts_ref[...].astype(F32), jnp.zeros((1, 128 - STRUCTS), F32)], axis=1)
    req_row = jnp.concatenate(
        [req_ref[...].reshape(1, NY * NZ * NC).astype(F32), jnp.zeros((1, 64), F32)], axis=1)
    sub, lane = iota((STRUCTS, 128), 0), iota((STRUCTS, 128), 1)
    counts_col = jnp.sum(jnp.where(sub == lane, counts_row, 0.0), axis=1, keepdims=True)
    starts_row = jnp.sum(jnp.where(sub < lane, counts_col, 0.0), axis=0, keepdims=True)
    starts_col = jnp.sum(jnp.where(lane < sub, counts_row, 0.0), axis=1, keepdims=True)
    info[...] = jnp.concatenate(
        [req_row, counts_row, starts_row, jnp.zeros((5, 128), F32)], axis=0)
    sizes[0] = info[...]

    pl.semaphore_wait(barrier, len(peers))

    def columns(j):
        return pl.ds(pl.multiple_of(j * FEATS, FEATS), FEATS)

    def hop(o, to, j):
        dst = lax.rem(o + to + NZ, NZ)
        copy(ring.at[o, :, columns(j)], ring.at[dst, :, columns(j)], z_send, z_recv.at[dst, j], at(to, 0, 0))

    def hop_sizes(o, to):
        dst = lax.rem(o + to + NZ, NZ)
        copy(sizes.at[o], sizes.at[dst], c_send, c_recv.at[dst], at(to, 0, 0))

    def move(d, e):
        copy(rows.at[pl.ds((e + d) % F * ROWS, ROWS), pl.ds(0, FEATS)],
             rows.at[pl.ds(e * ROWS, ROWS), pl.ds((F - d) * FEATS, FEATS)],
             x_send, x_recv.at[F - d if e == 0 else 0], feat_at(d))

    def halves(half):
        return pl.ds(half * ROWS // 4, ROWS // 4)

    def move_half(d, half):
        copy(rows.at[pl.ds(d * ROWS + half * ROWS // 4, ROWS // 4), pl.ds(0, FEATS)],
             rows.at[halves(half), pl.ds((F - d) * FEATS, FEATS)],
             x_send, xh_recv.at[F - d, half], feat_at(d))

    def enter_half(j, half):
        ring[0, halves(half), columns(j)] = rows[halves(half), columns(j)]
        for to in (1, NZ - 1):
            copy(ring.at[0, halves(half), columns(j)], ring.at[to, halves(half), columns(j)],
                 z_send, z_recv.at[to, j], at(1 if to == 1 else -1, 0, 0))

    def ask(dz, spots):
        for t in spots:
            dy, dc = NEAR[t]
            copy(info, asked.at[dz % 3 * SPOTS + t], a_send, a_recv.at[dz % 3], at(-dz, -dy, dc))

    def enter(j):
        ring[0, :, columns(j)] = rows[0:ROWS, columns(j)]
        hop(0, 1, j)
        hop(0, -1, j)

    enter(0)
    hop_sizes(0, 1)
    hop_sizes(0, -1)
    for half in range(4):
        move_half(F - 1, half)
        move_half(1, half)
    move(2, 0)
    ask(0, range(1, SPOTS))

    for j in BLOCKS[1:]:
        if j == 2:
            await_all(rows.at[pl.ds(0, ROWS), columns(j)], x_recv.at[j])
            enter(j)
        else:
            for half in range(4):
                await_all(rows.at[halves(half), columns(j)], xh_recv.at[j, half])
                enter_half(j, half)
        if j == BLOCKS[2]:
            for e in range(1, F):
                for d in (F - 1, 1, 2):
                    move(d, e)

    def pick(o, asks_rows):
        n = asks_rows.shape[0]
        sizes_ref = sizes.at[o]
        lanes = iota((n, 128), 1)
        asked_for = jnp.sum(jnp.where(lanes == struct_at(-o, 0, 0), asks_rows, 0.0), axis=1, keepdims=True)
        chosen = lanes.astype(F32) == asked_for
        count = jnp.sum(jnp.where(chosen, sizes_ref[1:2, :], 0.0), axis=1, keepdims=True)
        start = jnp.sum(jnp.where(chosen, sizes_ref[2:3, :], 0.0), axis=1, keepdims=True)
        begin = jnp.floor((start - ff + 3.0) * 0.25)
        end = jnp.floor((start + count - ff + 3.0) * 0.25)
        begin = jnp.broadcast_to(begin, (n, ROWS))
        end = jnp.broadcast_to(end, (n, ROWS))
        i, k = fiota((TILE, ROWS), 0), fiota((TILE, ROWS), 1)
        for t in range(n):
            chosen = (begin[t:t + 1] + i == k) & (k < end[t:t + 1])
            yield jnp.where(chosen, 1.0, 0.0).astype(BF16)

    def tile(n, t, j, to):
        part_rows = pl.ds(t * TILE, TILE)
        stage_rows = pl.ds(pl.multiple_of((n * SPOTS + t) * TILE, TILE), TILE)
        copy(stage.at[stage_rows, columns(j)], recv.at[n, part_rows, columns(j)], y_send, y_recv.at[n], to)

    def serve(o, n, j):
        made = dot(picks[o, 0:SPOTS * TILE], ring[o, :, columns(j)]).astype(BF16)
        stage[pl.ds(pl.multiple_of(n * SPOTS * TILE, TILE), SPOTS * TILE), columns(j)] = made
        recv[n, 0:TILE, columns(j)] = made[0:TILE]
        for t in range(1, SPOTS):
            tile(n, t, j, at(0, *NEAR[t]))

    def serve_far(o, down, j):
        made = dot(picks[o, SPOTS * TILE:], ring[o, :, columns(j)]).astype(BF16)
        for m in range(SPOTS // 2):
            t = 2 * m + down
            at_row = pl.multiple_of(t * TILE, TILE)
            n = NZ - 1
            stage_rows = pl.ds(pl.multiple_of(n * SPOTS * TILE + at_row, TILE), TILE)
            stage[stage_rows, columns(j)] = made[m * TILE:(m + 1) * TILE]
            copy(stage.at[stage_rows, columns(j)], recv.at[n, pl.ds(at_row, TILE), columns(j)],
                 y_send, y_recv.at[n], at(1 - 2 * down, m, down))

    def products(n):
        for b in range(ATOMS_DEV // WIDE):
            cols = slice(b * WIDE, (b + 1) * WIDE)
            p = lax.dot_general(recv[n], rows[cols, :], NT, preferred_element_type=F32)
            sums[pl.ds(pl.multiple_of(n * SPOTS, SPOTS), SPOTS), cols] = jnp.sum(
                (p * p).reshape(SPOTS, TILE, WIDE), axis=1)

    def near_products(n, carry):
        await_all(recv.at[n, pl.ds(TILE, (SPOTS - 1) * TILE)], y_recv.at[n])
        products(n)
        return carry

    def by_structure(first, last):
        return sum(
            lax.dot_general(inside[...], piece, NT, preferred_element_type=F32)
            for piece in split3(sums[first * SPOTS:last * SPOTS]))

    await_all(asked.at[pl.ds(0, SPOTS - 1)], a_recv.at[0])
    near_asks = jnp.concatenate([info[0:1, :]] + [asked[t, 0:1, :] for t in range(1, SPOTS)], axis=0)

    def pick_near(o):
        for t, chosen in enumerate(pick(o, near_asks)):
            picks[o, t * TILE:(t + 1) * TILE] = chosen

    pick_near(0)

    def own_block(j, carry):
        serve(0, 0, j)
        return carry

    lax.fori_loop(0, F, own_block, 0)

    column = iota((STRUCTS, ATOMS_DEV), 1)
    e_of = sum(jnp.where(column >= n * ROWS, 1, 0) for n in range(1, F))
    index = F * (column - ROWS * e_of) + lax.rem(f + e_of, F)
    index = index.astype(F32)
    belongs = (starts_col <= index) & (index < starts_col + counts_col)
    inside[...] = jnp.where(belongs, 1.0, 0.0).astype(BF16)
    seg_row = jnp.sum(jnp.where(belongs, fiota((STRUCTS, ATOMS_DEV), 0), 0.0), axis=0, keepdims=True)
    own_row = F * fiota((ROWS, 128), 0) + ff
    own_seg = jnp.sum(
        jnp.where((starts_row + counts_row <= own_row) & (iota((ROWS, 128), 1) < STRUCTS), 1.0, 0.0),
        axis=1, keepdims=True)

    def block_at(m):
        return jnp.where(m < 2, m, F + 1 - m)

    def next_hop(i, carry):
        hop_no, m = i // F + 1, lax.rem(i, F)
        j = block_at(m)

        def arrive(down, carry):
            o = jnp.where(down == 0, hop_no, NZ - hop_no)
            await_all(ring.at[o, :, columns(j)], z_recv.at[o, j])
            hop(o, 1 - 2 * down, j)

            @pl.when(m == 0)
            def _():
                await_all(sizes.at[o], c_recv.at[o])
                hop_sizes(o, 1 - 2 * down)
            return carry

        lax.fori_loop(0, 2, arrive, 0)

        @pl.when(i == 0)
        def _():
            ask(1, range(0, SPOTS, 2))
            ask(-1, range(1, SPOTS, 2))

        def send(down, carry):
            o = jnp.where(down == 0, hop_no, NZ - hop_no)

            @pl.when(m == 0)
            def _():
                pick_near(o)

            serve(o, 2 * hop_no - 1 + down, j)
            return carry

        lax.fori_loop(0, 2, send, 0)
        return carry

    lax.fori_loop(0, 2 * F, next_hop, 0)

    def self_kernel():
        total = jnp.zeros((STRUCTS, 1), F32)
        for b in range(ATOMS_DEV // WIDE):
            cols = slice(b * WIDE, (b + 1) * WIDE)
            p = lax.dot_general(rows[0:ROWS, :], rows[cols, :], NT, preferred_element_type=F32)
            p = jnp.where(own_seg == seg_row[:, cols], p, 0.0)
            by_column = jnp.sum(p * p, axis=0, keepdims=True)
            total = total + jnp.sum(
                jnp.where(inside[:, cols].astype(F32) > 0.5, by_column, 0.0), axis=1, keepdims=True)
        return total

    await_all(rows.at[pl.ds(ROWS, (F - 1) * ROWS), pl.ds(FEATS, (F - 1) * FEATS)], x_recv.at[0])
    self_col = self_kernel()
    own_self[...] = jnp.broadcast_to(
        jnp.sum(jnp.where(sub == lane, self_col, 0.0), axis=0, keepdims=True), (8, 128))
    for t in range(1, SPOTS):
        copy(own_self, near_self.at[t], s_send, s_recv, at(0, *NEAR[t]))

    def spread_self():
        await_all(near_self.at[pl.ds(1, SPOTS - 1)], s_recv)
        plane_self[...] = jnp.concatenate(
            [own_self[0:1, :]] + [near_self[t, 0:1, :] for t in range(1, SPOTS)], axis=0)
        for o in range(1, NZ):
            copy(plane_self, far_self.at[o], p_send, p_recv, at(o, 0, 0))

    def last_hop(m, carry):
        j = block_at(m)

        def send(down, carry):
            o = jnp.where(down == 0, 3, NZ - 3)
            await_all(ring.at[o, :, columns(j)], z_recv.at[o, j])

            @pl.when(m == 0)
            def _():
                await_all(sizes.at[o], c_recv.at[o])
                pick_near(o)
                await_all(asked.at[pl.ds(0, SPOTS // 2)], a_recv.at[1 + down])
                far_asks = jnp.concatenate(
                    [asked[(1 + down) * SPOTS + 2 * t + down, 0:1, :] for t in range(SPOTS // 2)], axis=0)
                for t, chosen in enumerate(pick(o, far_asks)):
                    picks[o, (SPOTS + t) * TILE:(SPOTS + t + 1) * TILE] = chosen

            serve_far(o, down, j)
            serve(o, 5 + down, j)
            return carry

        lax.fori_loop(0, 2, send, 0)

        @pl.when(m == 3)
        def _():
            spread_self()

        return carry

    lax.fori_loop(0, F, last_hop, 0)

    lax.fori_loop(0, EARLY, near_products, 0)
    early = by_structure(0, EARLY)

    def holder_of(spot):
        n = spot // SPOTS
        t = lax.rem(spot, SPOTS)
        o = sum(jnp.where(n == m, plane, 0) for m, plane in enumerate(PLANES))
        return (lax.rem(y - t // NC + NY, NY) * NZ + lax.rem(z - o + NZ, NZ)) * NC + lax.rem(
            c + lax.rem(t, NC), NC)

    holders = NZ * SPOTS
    spot, lanes = iota((holders, 128), 0), iota((holders, 128), 1)
    my_request = jnp.sum(jnp.where(lanes == holder_of(spot), info[0:1, :], 0.0), axis=1, keepdims=True)
    await_all(far_self.at[pl.ds(1, NZ - 1)], p_recv)
    all_self = jnp.concatenate([far_self[o] if o else plane_self[...] for o in PLANES], axis=0)
    partner_self = jnp.sum(jnp.where(lanes.astype(F32) == my_request, all_self, 0.0), axis=1, keepdims=True)
    partner_row = jnp.sum(jnp.where(lanes == spot, partner_self, 0.0), axis=0, keepdims=True)
    table[STRUCTS:STRUCTS + 8, :] = jnp.broadcast_to(partner_row, (8, 128))

    pairs = pl.ds(pl.multiple_of(f * PAIRS, 128), PAIRS)
    spot = iota((128, PAIRS), 0)
    slot_pick = jnp.where(
        (holder_of(spot) == slot_ref[pairs].reshape(1, PAIRS)) & (spot < holders), 1.0, 0.0).astype(BF16)
    local_pick = iota((STRUCTS, PAIRS), 0) == local_ref[pairs].reshape(1, PAIRS)

    lax.fori_loop(EARLY, NZ - 1, near_products, 0)
    await_all(recv.at[NZ - 1], y_recv.at[NZ - 1])
    products(NZ - 1)
    late = by_structure(EARLY, NZ)
    table[0:STRUCTS, :] = jnp.concatenate(
        [early, late, jnp.broadcast_to(self_col, (STRUCTS, 128 - holders))], axis=1)
    for d in range(1, F):
        copy(table, tables.at[d - 1], t_send, t_recv, feat_at(d))
    await_all(rows.at[:, pl.ds(FEATS, (F - 1) * FEATS)], x_send)
    await_all(ring.at[pl.ds(0, 6)], z_send)
    await_all(sizes.at[pl.ds(0, 6)], c_send)
    await_all(asked.at[pl.ds(0, 2 * SPOTS - 1)], a_send)
    await_all(stage.at[pl.ds(0, ((NZ - 1) * (SPOTS - 1) + SPOTS) * TILE)], y_send)
    await_all(near_self.at[pl.ds(0, SPOTS - 1)], s_send)
    await_all(far_self.at[pl.ds(0, NZ - 1)], p_send)
    await_all(tables, t_recv)
    await_all(tables, t_send)
    total = (table[...] + tables[0]) + (tables[1] + tables[2])
    picked = sum(dot(piece, slot_pick) for piece in split3(total))
    left_self = jnp.sum(jnp.where(local_pick, total[0:STRUCTS, holders:holders + 1], 0.0), axis=0, keepdims=True)
    value = jnp.sum(jnp.where(local_pick, picked[0:STRUCTS], 0.0), axis=0, keepdims=True)
    right_self = picked[STRUCTS:STRUCTS + 1]
    out_ref[...] = (value / jnp.sqrt(left_self * right_self)).reshape(PAIRS)


def per_device(descriptors, atom_counts, partner_requests, pair_local, pair_slot):
    dma = pltpu.SemaphoreType.DMA
    vmem = pltpu.VMEM

    inputs = (descriptors, atom_counts, partner_requests, pair_local, pair_slot)
    return pl.pallas_call(
        kernel,
        out_shape=jax.ShapeDtypeStruct((PAIRS,), F32),
        in_specs=[pl.BlockSpec(memory_space=pl.ANY)] * 5,
        out_specs=pl.BlockSpec(memory_space=vmem),
        scratch_shapes=[
            *[vmem(a.shape, a.dtype) for a in inputs],
            vmem((ATOMS_DEV, DEPTH), BF16),
            vmem((NZ, ROWS, DEPTH), BF16),
            vmem((NZ * SPOTS * TILE, DEPTH), BF16),
            vmem((NZ, SPOTS * TILE, DEPTH), BF16),
            vmem((NZ, (SPOTS + SPOTS // 2) * TILE, ROWS), BF16),
            vmem((8, 128), F32),
            vmem((3 * SPOTS, 8, 128), F32),
            vmem((NZ, 8, 128), F32),
            vmem((NZ * SPOTS, ATOMS_DEV), F32),
            vmem((STRUCTS, ATOMS_DEV), BF16),
            vmem((8, 128), F32),
            vmem((SPOTS, 8, 128), F32),
            vmem((8, 128), F32),
            vmem((NZ, 8, 128), F32),
            vmem((STRUCTS + 8, 128), F32),
            vmem((F - 1, STRUCTS + 8, 128), F32),
            dma((5,)), dma((F, 4)),
            dma(()), dma((F,)),
            dma(()), dma((NZ, F)),
            dma(()), dma((3,)),
            dma(()), dma((NZ,)),
            dma(()), dma((NZ,)),
            dma(()), dma(()),
            dma(()), dma(()),
            dma(()), dma(()),
        ],
        compiler_params=pltpu.CompilerParams(
            collective_id=0, has_side_effects=True, vmem_limit_bytes=62 * 1024 * 1024),
    )(*inputs)


def solution(mesh):
    in_specs = (P("struct", "feat"), P("struct", None), P("struct"), P("struct"), P("struct"))
    out_specs = P(("struct", "feat"))
    return jax.shard_map(
        per_device, mesh=mesh, in_specs=in_specs, out_specs=out_specs, check_vma=False)
```
